32 devices in a mesh: section: 4 (over y, core), expert: 8 (over z, x).
Axes of the slice: x: 2, y: 2, z: 4, core: 2. Of those that a mesh axis runs over, the one named last changes fastest.
Arguments:
- tokens_in: bfloat16 [8, 128, 2048], P(None, 'expert'), may hold values from -6 to 6
- expert_ids: int32 [4, 8, 128, 8], P('section'), may hold values from 0 to 7, as said below
- gate_values: float32 [4, 8, 128, 8], P('section', None, 'expert'), may hold values from 0.1 to 1
- expert_gate: bfloat16 [4, 8, 2048, 768], P('section', 'expert'), may hold values from -0.125 to 0.125
- expert_up: bfloat16 [4, 8, 2048, 768], P('section', 'expert'), may hold values from -0.125 to 0.125
- expert_down: bfloat16 [4, 8, 768, 2048], P('section', 'expert'), may hold values from -0.21875 to 0.21875
Outputs:
- layer_out: bfloat16 [4, 8, 128, 2048], P('section', None, 'expert')
The draws below stay inside these ranges and needn't reach their ends.
Inputs may be any that keep to these rules, and one draw needn't show every extreme that they name: `expert_ids`: every row names 8 different experts. In each layer and micro-batch the 16 rows of one device (aligned blocks) name no expert more than 16 times, and one expert is named exactly 16 times by the rows of every device.
All inputs are finite; a program needn't handle non-finite values.
Results may differ from the reference program's by a relative error of at most 0.025.
Values may be sent and summed in bfloat16 or wider, within the bound.
No kernel may reach another device: no remote copies, remote signals or barrier semaphores. Data moves between devices by JAX's collectives and lax.ppermute only.
A program may use at most 64 MiB of HBM per device.

```python
import math
import jax
import jax.numpy as jnp
from jax import lax

D = 2048
FF = 768
TOPK = 8
TOK_DEV = 16
MB = 8
LAYERS = 4
EXPERT_TOTAL = 8
TOKENS = 128
MOST = 16
N_EXPERT = 8


def draw_expert_ids(key, part):
    base_key = jax.random.fold_in(key, 7)
    hot_key, shuffle_key, quota_key, row_key = jax.random.split(base_key, 4)
    blocks = LAYERS * MB * N_EXPERT
    hot_expert = jnp.repeat(jax.random.randint(hot_key, (LAYERS * MB,), 0, EXPERT_TOTAL), N_EXPERT)
    shuffle_keys = jax.random.split(shuffle_key, blocks)
    rank_values = jax.vmap(lambda sub_key: jax.random.permutation(sub_key, EXPERT_TOTAL))(shuffle_keys).astype(jnp.int32)
    labels = jnp.arange(EXPERT_TOTAL, dtype=jnp.int32)
    is_hot = labels[None, :] == hot_expert[:, None]
    scores = jnp.where(is_hot, -1, rank_values)
    label_order = jnp.argsort(scores, axis=1).astype(jnp.int32)
    total_other = TOK_DEV * TOPK - MOST
    default_allotment = total_other // (EXPERT_TOTAL - 1)
    leftover_count = total_other % (EXPERT_TOTAL - 1)
    spread = max(0, min(default_allotment, MOST - default_allotment - 1))
    extra_units = jax.random.randint(quota_key, (blocks, EXPERT_TOTAL - 1), 0, spread + 1)
    adjustment_slots = extra_units - jnp.roll(extra_units, 1, axis=1)
    surplus_slots = (jnp.arange(EXPERT_TOTAL - 1) < leftover_count).astype(jnp.int32)
    allotment_remaining = default_allotment + surplus_slots[None, :] + adjustment_slots
    quotas = jnp.concatenate([jnp.full((blocks, 1), MOST, jnp.int32), allotment_remaining.astype(jnp.int32)], axis=1)
    quota_ends = jnp.cumsum(quotas, axis=1)
    slot_order = jnp.arange(TOK_DEV * TOPK, dtype=jnp.int32)
    position = jnp.sum((quota_ends[:, None, :] <= slot_order[None, :, None]).astype(jnp.int32), axis=2)
    chosen = jnp.take_along_axis(label_order, position, axis=1)
    id_grid = chosen.reshape(blocks, TOPK, TOK_DEV).transpose(0, 2, 1)
    row_keys = jax.random.split(row_key, blocks)
    sorted_row_index = jax.vmap(lambda sub_key: jax.random.permutation(sub_key, TOK_DEV))(row_keys)
    id_grid = jnp.take_along_axis(id_grid, sorted_row_index[:, :, None], axis=1)
    return id_grid.reshape(LAYERS, MB, N_EXPERT * TOK_DEV, TOPK).astype(jnp.int32)


def steps_of(stream_key, shape, cuts, low, top_value):
    loudness, own = 1.0, jax.random.fold_in(stream_key, 6)
    for axis_at, parts in cuts:
        heights = jnp.exp(jax.random.uniform(jax.random.fold_in(own, axis_at), (parts,), jnp.float32, low / len(cuts), top_value / len(cuts)))
        loudness = loudness * jnp.repeat(heights, shape[axis_at] // parts).reshape([-1 if axis == axis_at else 1 for axis in range(len(shape))])
    return loudness


def scatter_about(rng, dims, scale, most, shards=(), held_as=jnp.bfloat16):
    entries = jax.random.normal(rng, dims, jnp.float32) * scale
    if len(shards) > 0:
        entries = steps_of(rng, dims, shards, -0.22, 0.18) * entries
    return jnp.clip(entries, min=-most, max=most).astype(held_as)


def setup_inputs(seed: int = 0) -> dict:
    arg_keys = jax.random.split(jax.random.key(seed), 7)
    tokens_in = scatter_about(arg_keys[0], (MB, TOKENS, D), 1.0, 6.0, ((1, 8),))
    expert_ids = draw_expert_ids(jax.random.fold_in(arg_keys[6], 71), 0)
    gate_values = jnp.clip(jnp.exp(math.log(1.0) - 2.3025851 * jax.random.uniform(arg_keys[2], (LAYERS, MB, TOKENS, TOPK), jnp.float32) ** steps_of(arg_keys[2], (LAYERS, MB, TOKENS, TOPK), ((0, 4), (2, 8)), -0.2, 0.2)), 0.1, 1.0)
    expert_gate = scatter_about(arg_keys[3], (LAYERS, EXPERT_TOTAL, D, FF), D ** -0.5, 0.125, ((0, 4), (1, 8)))
    expert_up = scatter_about(arg_keys[4], (LAYERS, EXPERT_TOTAL, D, FF), D ** -0.5, 0.125, ((0, 4), (1, 8)))
    expert_down = scatter_about(arg_keys[5], (LAYERS, EXPERT_TOTAL, FF, D), FF ** -0.5, 0.21875, ((0, 4), (1, 8)))
    return {"tokens_in": tokens_in, "expert_ids": expert_ids, "gate_values": gate_values, "expert_gate": expert_gate, "expert_up": expert_up, "expert_down": expert_down}


epsilon = 1e-06

def apply_expert(operands):
    row_block, gate_matrix, up_matrix, down_matrix = operands
    widened_rows = row_block.astype(jnp.float32)
    gate_part = jnp.dot(widened_rows, gate_matrix.astype(jnp.float32), preferred_element_type=jnp.float32)
    up_part = jnp.dot(widened_rows, up_matrix.astype(jnp.float32), preferred_element_type=jnp.float32)
    activated = (jax.nn.silu(gate_part) * up_part).astype(jnp.bfloat16)
    return jnp.dot(activated.astype(jnp.float32), down_matrix.astype(jnp.float32), preferred_element_type=jnp.float32).astype(jnp.bfloat16)

def expert_layer(hidden, route_ids, gate_rows, stacked_gate_weights, up_stack, down_stack):
    widened = hidden.reshape(MB * TOKENS, D).astype(jnp.float32)
    normed = (widened * lax.rsqrt(lax.optimization_barrier(jnp.mean(widened * widened, axis=-1, keepdims=True)) + epsilon)).astype(jnp.bfloat16)
    slot_capacity = MB * N_EXPERT * MOST
    flat_ids = route_ids.reshape(MB * TOKENS * TOPK).astype(jnp.int32)
    onehot = (flat_ids[:, None] == jnp.arange(EXPERT_TOTAL, dtype=jnp.int32)[None, :]).astype(jnp.int32)
    ahead_count = (jnp.cumsum(onehot, axis=0) - onehot).astype(jnp.int32)
    place_in = lax.optimization_barrier(jnp.sum(ahead_count * onehot, axis=1)).astype(jnp.int32)
    target = (flat_ids * slot_capacity + place_in).astype(jnp.int32)
    owner_row = (jnp.arange(MB * TOKENS * TOPK, dtype=jnp.int32) // TOPK).astype(jnp.int32)
    source = jnp.full((EXPERT_TOTAL * slot_capacity,), MB * TOKENS, jnp.int32).at[target].set(owner_row)
    padded = jnp.concatenate([normed, jnp.zeros((1, D), jnp.bfloat16)], axis=0)
    grouped = padded[source].reshape(EXPERT_TOTAL, slot_capacity, D)
    results = lax.map(apply_expert, (grouped, stacked_gate_weights, up_stack, down_stack)).reshape(EXPERT_TOTAL * slot_capacity, D)
    picked = results[target].reshape(MB * TOKENS, TOPK, D).astype(jnp.float32)
    weights_flat = gate_rows.reshape(MB * TOKENS, TOPK).astype(jnp.float32)
    combined = widened + lax.optimization_barrier(jnp.sum(weights_flat[:, :, None] * picked, axis=1))
    return combined.astype(jnp.bfloat16).reshape(MB, TOKENS, D)

def reference(tokens_in, expert_ids, gate_values, expert_gate, expert_up, expert_down):
    collected = []
    hidden = tokens_in
    for layer_index in range(LAYERS):
        hidden = expert_layer(hidden, expert_ids[layer_index], gate_values[layer_index], expert_gate[layer_index], expert_up[layer_index], expert_down[layer_index])
        collected.append(hidden)
    return jnp.stack(collected)
```

```python
import functools

import jax
import jax.numpy as jnp
from jax import lax
from jax.experimental import pallas as pl
from jax.experimental.pallas import tpu as pltpu
from jax.sharding import PartitionSpec as P

epsilon = 1e-06
hidden_tile = 256


def mlp_kernel(own_ref, other_ref, weight_ref, gate_ref, up_ref, down_ref, keep_ref, give_ref, normed_ref, total_ref):
    step = pl.program_id(0)
    half = own_ref.shape[0]

    @pl.when(step == 0)
    def _():
        for place, rows_ref in enumerate((own_ref, other_ref)):
            widened = rows_ref[...].astype(jnp.float32)
            inverse_rms = lax.rsqrt(jnp.mean(widened * widened, axis=-1, keepdims=True) + epsilon)
            normed_ref[place * half : (place + 1) * half, :] = (widened * inverse_rms).astype(jnp.bfloat16)

    normed = normed_ref[...]
    gate_part = jnp.dot(normed, gate_ref[...], preferred_element_type=jnp.float32)
    up_part = jnp.dot(normed, up_ref[...], preferred_element_type=jnp.float32)
    activated = (gate_part / (1.0 + jnp.exp(-gate_part)) * up_part).astype(jnp.bfloat16)
    partial = jnp.dot(activated, down_ref[...], preferred_element_type=jnp.float32)

    @pl.when(step == 0)
    def _():
        total_ref[...] = partial

    @pl.when(step > 0)
    def _():
        total_ref[...] += partial

    @pl.when(step == pl.num_programs(0) - 1)
    def _():
        weighted = total_ref[...] * weight_ref[...]
        keep_ref[...] = weighted[:half].astype(jnp.bfloat16)
        give_ref[...] = weighted[half:].astype(jnp.bfloat16)


def expert_mlp(own, other, weights, gate_matrix, up_matrix, down_matrix):
    half, features = own.shape
    rows = 2 * half
    hidden = gate_matrix.shape[1]
    whole = lambda j: (0, 0)
    return pl.pallas_call(
        mlp_kernel,
        grid=(hidden // hidden_tile,),
        in_specs=[
            pl.BlockSpec((half, features), whole),
            pl.BlockSpec((half, features), whole),
            pl.BlockSpec((rows, 1), whole),
            pl.BlockSpec((features, hidden_tile), lambda j: (0, j)),
            pl.BlockSpec((features, hidden_tile), lambda j: (0, j)),
            pl.BlockSpec((hidden_tile, features), lambda j: (j, 0)),
        ],
        out_specs=[pl.BlockSpec((half, features), whole), pl.BlockSpec((half, features), whole)],
        out_shape=[jax.ShapeDtypeStruct((half, features), jnp.bfloat16)] * 2,
        scratch_shapes=[pltpu.VMEM((rows, features), jnp.bfloat16), pltpu.VMEM((rows, features), jnp.float32)],
        compiler_params=pltpu.CompilerParams(vmem_limit_bytes=40 * 1024 * 1024),
        cost_estimate=pl.CostEstimate(
            flops=6 * rows * features * hidden, bytes_accessed=6 * features * hidden, transcendentals=rows * hidden
        ),
        name="expert_mlp",
    )(own, other, weights, gate_matrix, up_matrix, down_matrix)


def body(tokens_in, expert_ids, gate_values, expert_gate, expert_up, expert_down):
    sections = lax.axis_size("section")
    section_now = lax.axis_index("section")
    experts = lax.axis_size("expert")
    my_expert = lax.axis_index("expert")
    columns = experts // 2
    my_column, my_side = my_expert // 2, my_expert % 2
    batches, row_count, features = tokens_in.shape
    gate_matrix, up_matrix, down_matrix = expert_gate[0, 0], expert_up[0, 0], expert_down[0, 0]
    half = columns * row_count

    my_routes = lax.dynamic_slice_in_dim(expert_ids[0], my_expert * row_count, row_count, 1)
    named = my_routes[None] == jnp.arange(experts, dtype=jnp.int32)[:, None, None, None]
    token_weights = jnp.sum(jnp.where(named, gate_values[0][None], 0.0), axis=3)
    token_weights = lax.all_to_all(token_weights, "expert", split_axis=0, concat_axis=0, tiled=True)
    apart = jnp.arange(columns, dtype=jnp.int32)
    sources = (my_column - apart) % columns * 2
    order = jnp.concatenate([sources + my_side, sources + 1 - my_side])
    token_weights = token_weights[order].transpose(1, 0, 2).reshape(batches, 2 * half, 1)

    def along_columns(block, apart, active, source_step):
        route = []
        for section in active:
            for column in range(columns):
                for side in range(2):
                    source = (section - source_step) % sections * experts + column * 2 + side
                    route.append((source, section * experts + (column + apart) % columns * 2 + side))
        return lax.ppermute(block, ("section", "expert"), route)

    def across(block, active):
        route = [(s * experts + e, s * experts + (e ^ 1)) for s in active for e in range(experts)]
        return lax.ppermute(block, ("section", "expert"), route)

    def added(*terms):
        return functools.reduce(jnp.add, [term.astype(jnp.float32) for term in terms])

    slots = 2 * sections + batches - 1
    results = []
    result = None
    second_half = None
    for slot in range(slots):
        opening = [s for s in range(sections) if 0 <= slot - 2 * s < batches]
        closing = [s for s in range(sections) if 0 <= slot - 2 * s - 1 < batches]
        if opening:
            fresh = tokens_in[min(slot, batches - 1)]
            payload = fresh if result is None else jnp.where(section_now == sections - 1, fresh, result)
            gathered = [along_columns(payload, d, opening, 1) for d in range(columns)]
        if closing:
            residual, keep, give = second_half
            received = across(give, closing)
            summed = added(keep, received).astype(jnp.bfloat16).reshape(columns, row_count, features)
            returned = [along_columns(summed[d], -d, closing, 0) for d in range(1, columns)]
            result = added(residual, summed[0], *returned).astype(jnp.bfloat16)
            results.append(result)
        if opening:
            own = jnp.concatenate(gathered, axis=0)
            other = across(own, opening)
            round_now = jnp.clip(slot - 2 * section_now, 0, batches - 1)
            weights = lax.dynamic_index_in_dim(token_weights, round_now, 0, keepdims=False)
            keep, give = expert_mlp(own, other, weights, gate_matrix, up_matrix, down_matrix)
            second_half = (gathered[0], keep, give)
    outputs = lax.dynamic_slice_in_dim(jnp.stack(results), 2 * section_now, batches, 0)
    return outputs[None]


def solution(mesh):
    return jax.shard_map(
        body,
        mesh=mesh,
        in_specs=(
            P(None, "expert", None),
            P("section", None, None, None),
            P("section", None, "expert", None),
            P("section", "expert", None, None),
            P("section", "expert", None, None),
            P("section", "expert", None, None),
        ),
        out_specs=P("section", None, "expert", None),
        check_vma=False,
    )
```

```python
import functools

import jax
import jax.numpy as jnp
from jax import lax
from jax.experimental import pallas as pl
from jax.experimental.pallas import tpu as pltpu
from jax.sharding import PartitionSpec as P

epsilon = 1e-06
hidden_tile = 256
unrolled_experts = 8


def mlp_kernel(
    own_ref, other_ref, weight_ref, gate_hbm, up_hbm, down_hbm, keep_ref, give_ref,
    gate_ref, up_ref, down_ref, normed_ref, total_ref, arrived,
):
    half = own_ref.shape[0]
    tiles = gate_hbm.shape[1] // hidden_tile
    copies = []
    for tile in range(tiles):
        place = pl.ds(tile * hidden_tile, hidden_tile)
        copies.append(
            (
                pltpu.make_async_copy(gate_hbm.at[:, place], gate_ref.at[tile], arrived.at[tile, 0]),
                pltpu.make_async_copy(up_hbm.at[:, place], up_ref.at[tile], arrived.at[tile, 1]),
                pltpu.make_async_copy(down_hbm.at[place, :], down_ref.at[tile], arrived.at[tile, 2]),
            )
        )
    for group in copies:
        for copy in group:
            copy.start()
    for side, rows_ref in enumerate((own_ref, other_ref)):
        widened = rows_ref[...].astype(jnp.float32)
        inverse_rms = lax.rsqrt(jnp.mean(widened * widened, axis=-1, keepdims=True) + epsilon)
        normed_ref[side * half : (side + 1) * half, :] = (widened * inverse_rms).astype(jnp.bfloat16)
    normed = normed_ref[...]
    for tile in range(tiles):
        copies[tile][0].wait()
        gate_part = jnp.dot(normed, gate_ref[tile], preferred_element_type=jnp.float32)
        copies[tile][1].wait()
        up_part = jnp.dot(normed, up_ref[tile], preferred_element_type=jnp.float32)
        activated = (gate_part / (1.0 + jnp.exp(-gate_part)) * up_part).astype(jnp.bfloat16)
        copies[tile][2].wait()
        partial = jnp.dot(activated, down_ref[tile], preferred_element_type=jnp.float32)
        if tile == 0:
            total_ref[...] = partial
        else:
            total_ref[...] += partial
    weighted = total_ref[...] * weight_ref[...]
    keep_ref[...] = weighted[:half].astype(jnp.bfloat16)
    give_ref[...] = weighted[half:].astype(jnp.bfloat16)


def expert_mlp(own, other, weights, gate_matrix, up_matrix, down_matrix):
    half, features = own.shape
    rows = 2 * half
    hidden = gate_matrix.shape[1]
    tiles = hidden // hidden_tile
    in_vmem = pl.BlockSpec(memory_space=pltpu.VMEM)
    in_hbm = pl.BlockSpec(memory_space=pltpu.HBM)
    return pl.pallas_call(
        mlp_kernel,
        in_specs=[in_vmem] * 3 + [in_hbm] * 3,
        out_specs=[in_vmem] * 2,
        out_shape=[jax.ShapeDtypeStruct((half, features), jnp.bfloat16)] * 2,
        scratch_shapes=[
            pltpu.VMEM((tiles, features, hidden_tile), jnp.bfloat16),
            pltpu.VMEM((tiles, features, hidden_tile), jnp.bfloat16),
            pltpu.VMEM((tiles, hidden_tile, features), jnp.bfloat16),
            pltpu.VMEM((rows, features), jnp.bfloat16),
            pltpu.VMEM((rows, features), jnp.float32),
            pltpu.SemaphoreType.DMA((tiles, 3)),
        ],
        compiler_params=pltpu.CompilerParams(vmem_limit_bytes=40 * 1024 * 1024),
        cost_estimate=pl.CostEstimate(
            flops=6 * rows * features * hidden, bytes_accessed=6 * features * hidden, transcendentals=rows * hidden
        ),
        name="expert_mlp",
    )(own, other, weights, gate_matrix, up_matrix, down_matrix)


def body(tokens_in, expert_ids, gate_values, expert_gate, expert_up, expert_down):
    sections = lax.axis_size("section")
    section_now = lax.axis_index("section")
    experts = lax.axis_size("expert")
    my_expert = lax.axis_index("expert")
    columns = experts // 2
    my_column, my_side = my_expert // 2, my_expert % 2
    batches, row_count, features = tokens_in.shape
    gate_matrix, up_matrix, down_matrix = expert_gate[0, 0], expert_up[0, 0], expert_down[0, 0]
    half = columns * row_count

    my_routes = lax.dynamic_slice_in_dim(expert_ids[0], my_expert * row_count, row_count, 1)
    named = my_routes[None] == jnp.arange(experts, dtype=jnp.int32)[:, None, None, None]
    token_weights = jnp.sum(jnp.where(named, gate_values[0][None], 0.0), axis=3)
    token_weights = lax.all_to_all(token_weights, "expert", split_axis=0, concat_axis=0, tiled=True)
    apart = jnp.arange(columns, dtype=jnp.int32)
    sources = (my_column - apart) % columns * 2
    order = jnp.concatenate([sources + my_side, sources + 1 - my_side])
    token_weights = token_weights[order].transpose(1, 0, 2).reshape(batches, 2 * half, 1)

    def along_columns(block, apart, source_step):
        route = []
        for section in range(sections):
            for column in range(columns):
                for side in range(2):
                    source = (section - source_step) % sections * experts + column * 2 + side
                    route.append((source, section * experts + (column + apart) % columns * 2 + side))
        return lax.ppermute(block, ("section", "expert"), route)

    def across(block):
        return lax.ppermute(block, "expert", [(e, e ^ 1) for e in range(experts)])

    def added(*terms):
        return functools.reduce(jnp.add, [term.astype(jnp.float32) for term in terms])

    def one_slot(slot, state, opening=True, closing=True):
        result, residual, keep, give = state
        if opening:
            fresh = lax.dynamic_index_in_dim(tokens_in, jnp.minimum(slot, batches - 1), 0, keepdims=False)
            payload = fresh if result is None else jnp.where(section_now == sections - 1, fresh, result)
            gathered = [along_columns(payload, d, 1) for d in range(columns)]
        if closing:
            received = across(give)
            summed = added(keep, received).astype(jnp.bfloat16).reshape(columns, row_count, features)
            returned = [along_columns(summed[d], -d, 0) for d in range(1, columns)]
            result = added(residual, summed[0], *returned).astype(jnp.bfloat16)
        if opening:
            own = jnp.concatenate(gathered, axis=0)
            other = across(own)
            round_now = jnp.clip(slot - 2 * section_now, 0, batches - 1)
            weights = lax.dynamic_index_in_dim(token_weights, round_now, 0, keepdims=False)
            residual = gathered[0]
            keep, give = expert_mlp(own, other, weights, gate_matrix, up_matrix, down_matrix)
        return (result, residual, keep, give)

    slots = 2 * sections + batches - 1
    state = (None, None, None, None)
    if experts <= unrolled_experts:
        results = []
        for slot in range(slots):
            state = one_slot(slot, state, slot < slots - 1, slot > 0)
            results.append(state[0])
        results = jnp.stack(results[1:])
    else:
        blank = jnp.zeros((half, features), jnp.bfloat16)
        rows_blank = jnp.zeros((row_count, features), jnp.bfloat16)

        def looped(slot, carried):
            state = one_slot(slot, carried[0])
            return state, lax.dynamic_update_index_in_dim(carried[1], state[0], slot, 0)

        kept = jnp.zeros((slots, row_count, features), jnp.bfloat16)
        results = lax.fori_loop(0, slots, looped, ((rows_blank, rows_blank, blank, blank), kept))[1][1:]
    return lax.dynamic_slice_in_dim(results, 2 * section_now, batches, 0)[None]


def solution(mesh):
    return jax.shard_map(
        body,
        mesh=mesh,
        in_specs=(
            P(None, "expert", None),
            P("section", None, None, None),
            P("section", None, "expert", None),
            P("section", "expert", None, None),
            P("section", "expert", None, None),
            P("section", "expert", None, None),
        ),
        out_specs=P("section", None, "expert", None),
        check_vma=False,
    )
```

```python
import functools

import jax
import jax.numpy as jnp
from jax import lax
from jax.experimental import pallas as pl
from jax.experimental.pallas import tpu as pltpu
from jax.sharding import PartitionSpec as P

epsilon = 1e-06
group = 1
unrolled_experts = 8


def mlp_kernel(own_ref, other_ref, weight_ref, gate_ref, up_ref, down_ref, keep_ref, give_ref, normed_ref):
    half = own_ref.shape[0]
    for side, rows_ref in enumerate((own_ref, other_ref)):
        widened = rows_ref[...].astype(jnp.float32)
        inverse_rms = lax.rsqrt(jnp.mean(widened * widened, axis=-1, keepdims=True) + epsilon)
        normed_ref[side * half : (side + 1) * half, :] = (widened * inverse_rms).astype(jnp.bfloat16)
    gate_part = jnp.dot(normed_ref[...], gate_ref[...], preferred_element_type=jnp.float32)
    up_part = jnp.dot(normed_ref[...], up_ref[...], preferred_element_type=jnp.float32)
    activated = (gate_part / (1.0 + jnp.exp(-gate_part)) * up_part).astype(jnp.bfloat16)
    weighted = jnp.dot(activated, down_ref[...], preferred_element_type=jnp.float32) * weight_ref[...]
    keep_ref[...] = weighted[:half].astype(jnp.bfloat16)
    give_ref[...] = weighted[half:].astype(jnp.bfloat16)


def expert_mlp(own, other, weights, gate_matrix, up_matrix, down_matrix):
    half, features = own.shape
    rows = 2 * half
    hidden = gate_matrix.shape[1]
    in_vmem = pl.BlockSpec(memory_space=pltpu.VMEM)
    return pl.pallas_call(
        mlp_kernel,
        in_specs=[in_vmem] * 6,
        out_specs=[in_vmem] * 2,
        out_shape=[jax.ShapeDtypeStruct((half, features), jnp.bfloat16)] * 2,
        scratch_shapes=[pltpu.VMEM((rows, features), jnp.bfloat16)],
        compiler_params=pltpu.CompilerParams(vmem_limit_bytes=24 * 1024 * 1024),
        cost_estimate=pl.CostEstimate(
            flops=6 * rows * features * hidden, bytes_accessed=6 * features * hidden, transcendentals=rows * hidden
        ),
        name="expert_mlp",
    )(own, other, weights, gate_matrix, up_matrix, down_matrix)


def body(tokens_in, expert_ids, gate_values, expert_gate, expert_up, expert_down):
    sections = lax.axis_size("section")
    section_now = lax.axis_index("section")
    experts = lax.axis_size("expert")
    my_expert = lax.axis_index("expert")
    columns = experts // 2
    my_column, my_side = my_expert // 2, my_expert % 2
    batches, row_count, features = tokens_in.shape
    gate_matrix, up_matrix, down_matrix = (
        pltpu.with_memory_space_constraint(matrix[0, 0], pltpu.VMEM) for matrix in (expert_gate, expert_up, expert_down)
    )
    rounds = batches // group
    block = group * row_count
    half = columns * block

    my_routes = lax.dynamic_slice_in_dim(expert_ids[0], my_expert * row_count, row_count, 1)
    named = my_routes[None] == jnp.arange(experts, dtype=jnp.int32)[:, None, None, None]
    token_weights = jnp.sum(jnp.where(named, gate_values[0][None], 0.0), axis=3)
    token_weights = lax.all_to_all(token_weights, "expert", split_axis=0, concat_axis=0, tiled=True)
    apart = jnp.arange(columns, dtype=jnp.int32)
    sources = (my_column - apart) % columns * 2
    order = jnp.concatenate([sources + my_side, sources + 1 - my_side])
    token_weights = token_weights[order].reshape(experts, rounds, block).transpose(1, 0, 2).reshape(rounds, 2 * half, 1)

    def along_columns(block, apart, source_step):
        route = []
        for section in range(sections):
            for column in range(columns):
                for side in range(2):
                    source = (section - source_step) % sections * experts + column * 2 + side
                    route.append((source, section * experts + (column + apart) % columns * 2 + side))
        return lax.ppermute(block, ("section", "expert"), route)

    def across(block):
        return lax.ppermute(block, "expert", [(e, e ^ 1) for e in range(experts)])

    def added(*terms):
        return functools.reduce(jnp.add, [term.astype(jnp.float32) for term in terms])

    fresh_rounds = tokens_in.reshape(rounds, block, features)

    def one_slot(slot, state, opening=True, closing=True):
        result, own, other = state
        if closing:
            round_now = jnp.clip(slot - 1 - 2 * section_now, 0, rounds - 1)
            weights = lax.dynamic_index_in_dim(token_weights, round_now, 0, keepdims=False)
            residual = own[:block]
            keep, give = expert_mlp(own, other, weights, gate_matrix, up_matrix, down_matrix)
        if opening:
            fresh = lax.dynamic_index_in_dim(fresh_rounds, jnp.minimum(slot, rounds - 1), 0, keepdims=False)
            payload = fresh if result is None else jnp.where(section_now == sections - 1, fresh, result)
            if closing:
                give, payload = lax.optimization_barrier((give, payload))
            gathered = [along_columns(payload, d, 1) for d in range(columns)]
        if closing:
            received = across(give)
            summed = added(keep, received).astype(jnp.bfloat16).reshape(columns, block, features)
            returned = [along_columns(summed[d], -d, 0) for d in range(1, columns)]
            result = added(residual, summed[0], *returned).astype(jnp.bfloat16)
        if opening:
            own = jnp.concatenate(gathered, axis=0)
            other = across(own)
        return (result, own, other)

    slots = 2 * sections + rounds - 1
    state = (None, None, None)
    if experts <= unrolled_experts:
        results = []
        for slot in range(slots):
            state = one_slot(slot, state, slot < slots - 1, slot > 0)
            results.append(state[0])
        results = jnp.stack(results[1:])
    else:
        blank = jnp.zeros((half, features), jnp.bfloat16)
        rows_blank = jnp.zeros((block, features), jnp.bfloat16)

        def looped(slot, carried):
            state = one_slot(slot, carried[0])
            return state, lax.dynamic_update_index_in_dim(carried[1], state[0], slot, 0)

        kept = jnp.zeros((slots, block, features), jnp.bfloat16)
        results = lax.fori_loop(0, slots, looped, ((rows_blank, blank, blank), kept))[1][1:]
    results = lax.dynamic_slice_in_dim(results, 2 * section_now, rounds, 0)
    return results.reshape(1, batches, row_count, features)


def solution(mesh):
    return jax.shard_map(
        body,
        mesh=mesh,
        in_specs=(
            P(None, "expert", None),
            P("section", None, None, None),
            P("section", None, "expert", None),
            P("section", "expert", None, None),
            P("section", "expert", None, None),
            P("section", "expert", None, None),
        ),
        out_specs=P("section", None, "expert", None),
        check_vma=False,
    )
```

```python
import functools

import jax
import jax.numpy as jnp
from jax import lax
from jax.experimental import pallas as pl
from jax.experimental.pallas import tpu as pltpu
from jax.sharding import PartitionSpec as P

epsilon = 1e-06
group = 1
unrolled_experts = 8


def mlp_kernel(
    pick_ref, own_ref, other_ref, weight_ref, gate_0, up_0, down_0, gate_1, up_1, down_1, keep_ref, give_ref, normed_ref
):
    half = own_ref.shape[0]
    for side, rows_ref in enumerate((own_ref, other_ref)):
        widened = rows_ref[...].astype(jnp.float32)
        inverse_rms = lax.rsqrt(jnp.mean(widened * widened, axis=-1, keepdims=True) + epsilon)
        normed_ref[side * half : (side + 1) * half, :] = (widened * inverse_rms).astype(jnp.bfloat16)

    def with_weights(gate_ref, up_ref, down_ref):
        gate_part = jnp.dot(normed_ref[...], gate_ref[...], preferred_element_type=jnp.float32)
        up_part = jnp.dot(normed_ref[...], up_ref[...], preferred_element_type=jnp.float32)
        activated = (gate_part / (1.0 + jnp.exp(-gate_part)) * up_part).astype(jnp.bfloat16)
        row_weights = jnp.broadcast_to(weight_ref[pick_ref[0], pick_ref[1]], (128, 2 * half)).T[:, :1]
        weighted = jnp.dot(activated, down_ref[...], preferred_element_type=jnp.float32) * row_weights
        keep_ref[...] = weighted[:half].astype(jnp.bfloat16)
        give_ref[...] = weighted[half:].astype(jnp.bfloat16)

    @pl.when(pick_ref[0] == 0)
    def _():
        with_weights(gate_0, up_0, down_0)

    @pl.when(pick_ref[0] == 1)
    def _():
        with_weights(gate_1, up_1, down_1)


def expert_mlp(pick, own, other, token_weights, matrices):
    half, features = own.shape
    rows = 2 * half
    hidden = matrices[0].shape[1]
    in_vmem = pl.BlockSpec(memory_space=pltpu.VMEM)
    return pl.pallas_call(
        mlp_kernel,
        in_specs=[pl.BlockSpec(memory_space=pltpu.SMEM)] + [in_vmem] * 9,
        out_specs=[in_vmem] * 2,
        out_shape=[jax.ShapeDtypeStruct((half, features), jnp.bfloat16)] * 2,
        scratch_shapes=[pltpu.VMEM((rows, features), jnp.bfloat16)],
        compiler_params=pltpu.CompilerParams(vmem_limit_bytes=(8 << 20) + 28 * rows * features),
        cost_estimate=pl.CostEstimate(
            flops=6 * rows * features * hidden, bytes_accessed=6 * features * hidden, transcendentals=rows * hidden
        ),
        name="expert_mlp",
    )(pick, own, other, token_weights, *matrices)


def body(tokens_in, expert_ids, gate_values, expert_gate, expert_up, expert_down):
    sections = lax.axis_size("section")
    section_now = lax.axis_index("section")
    experts = lax.axis_size("expert")
    my_expert = lax.axis_index("expert")
    planes = sections // 2
    my_plane, my_core = section_now // 2, section_now % 2
    columns = experts // 2
    my_column, my_side = my_expert // 2, my_expert % 2
    batches, row_count, features = tokens_in.shape
    block = group * row_count
    half = columns * block
    rounds = batches // (2 * group)
    pairs = rounds // 2

    def swapped(value):
        return lax.ppermute(value, "section", [(s, s ^ 1) for s in range(sections)])

    own_matrices = (expert_gate[0, 0], expert_up[0, 0], expert_down[0, 0])
    matrices = own_matrices + tuple(swapped(matrix) for matrix in own_matrices)
    matrices = tuple(pltpu.with_memory_space_constraint(matrix, pltpu.VMEM) for matrix in matrices)

    my_routes = lax.dynamic_slice_in_dim(expert_ids[0], my_expert * row_count, row_count, 1)
    named = my_routes[None] == jnp.arange(experts, dtype=jnp.int32)[:, None, None, None]
    token_weights = jnp.sum(jnp.where(named, gate_values[0][None], 0.0), axis=3)
    token_weights = lax.all_to_all(token_weights, "expert", split_axis=0, concat_axis=0, tiled=True)
    apart = jnp.arange(columns, dtype=jnp.int32)
    sources = (my_column - apart) % columns * 2
    order = jnp.concatenate([sources + my_side, sources + 1 - my_side])
    token_weights = token_weights[order].reshape(experts, rounds, 2, block).transpose(2, 1, 0, 3)
    token_weights = token_weights.reshape(2, rounds, 1, 2 * half)
    kept = lax.dynamic_index_in_dim(token_weights, my_core, 0, keepdims=False)
    sent = lax.dynamic_index_in_dim(token_weights, 1 - my_core, 0, keepdims=False)
    token_weights = jnp.stack([kept, swapped(sent)])

    fresh_rounds = lax.dynamic_index_in_dim(
        tokens_in.reshape(rounds, 2, block, features), my_core, 1, keepdims=False
    )

    def along_columns(value, apart, planes_on):
        route = []
        for section in range(sections):
            for e in range(experts):
                target = (section + 2 * planes_on) % sections * experts + (e // 2 + apart) % columns * 2 + e % 2
                route.append((section * experts + e, target))
        return lax.ppermute(value, ("section", "expert"), route)

    def across(value):
        return lax.ppermute(value, "expert", [(e, e ^ 1) for e in range(experts)])

    def added(*terms):
        return functools.reduce(jnp.add, [term.astype(jnp.float32) for term in terms])

    def one_slot(opening, closing):
        opened = result = None
        if closing is not None:
            own, other, layer, round_now = closing
            pick = jnp.stack([(layer + my_core) % 2, round_now]).astype(jnp.int32)
            keep, give = expert_mlp(pick, own, other, token_weights, matrices)
        if opening is not None:
            payload, from_before = opening
            if closing is not None:
                give, payload = lax.optimization_barrier((give, payload))
            first = along_columns(payload, 0, 1) if from_before else payload
            gathered = [first] + [along_columns(payload, d, int(from_before)) for d in range(1, columns)]
        if closing is not None:
            summed = added(keep, across(give)).astype(jnp.bfloat16).reshape(columns, block, features)
            returned = [along_columns(summed[d], -d, 0) for d in range(1, columns)]
            result = added(own[:block], summed[0], *returned).astype(jnp.bfloat16)
        if opening is not None:
            own_column = jnp.concatenate(gathered, axis=0)
            opened = (own_column, across(own_column))
        return opened, result

    steps = planes + pairs - 1

    def one_step(step, result_a, second_b, first=False):
        pair = jnp.clip(step - my_plane, 0, pairs - 1)
        pair_before = jnp.clip(step - 1 - my_plane, 0, pairs - 1)
        entering = jnp.minimum(step, pairs - 1) * 2
        fresh = [lax.dynamic_index_in_dim(fresh_rounds, entering + i, 0, keepdims=False) for i in range(2)]

        def payload(rows, i):
            return fresh[i] if rows is None else jnp.where(my_plane == planes - 1, fresh[i], rows)

        closing = None if first else (*second_b, 1, pair_before * 2 + 1)
        opened_a, last_b = one_slot((payload(result_a, 0), not first), closing)
        opened_b, first_a = one_slot((payload(last_b, 1), not first), (*opened_a, 0, pair * 2))
        opened_a, first_b = one_slot((first_a, False), (*opened_b, 0, pair * 2 + 1))
        opened_b, last_a = one_slot((first_b, False), (*opened_a, 1, pair * 2))
        return (first_a, last_a, first_b, last_b), opened_b

    if experts <= unrolled_experts:
        history, result_a, second_b = [], None, None
        for step in range(steps):
            results, second_b = one_step(step, result_a, second_b, step == 0)
            result_a = results[1]
            history.append(results)
        last_b = one_slot(None, (*second_b, 1, pairs * 2 - 1))[1]
        late_b = [results[3] for results in history[1:]] + [last_b]
        history = [jnp.stack(part) for part in (*list(zip(*history))[:3], late_b)]
    else:
        blank, rows_blank = jnp.zeros((half, features), jnp.bfloat16), jnp.zeros((block, features), jnp.bfloat16)

        def looped(step, carried):
            results, second_b = one_step(step, *carried[:2])
            history = [lax.dynamic_update_index_in_dim(h, r, step, 0) for h, r in zip(carried[2], results)]
            return results[1], second_b, history

        kept = [jnp.zeros((steps + 1, block, features), jnp.bfloat16)] * 4
        carried = lax.fori_loop(0, steps + 1, looped, (rows_blank, (blank, blank), kept))
        history = [h[:-1] for h in carried[2][:3]] + [carried[2][3][1:]]
    history = [lax.dynamic_slice_in_dim(h, my_plane, pairs, 0) for h in history]
    layers = [jnp.stack([history[i], history[i + 2]], axis=1) for i in range(2)]
    kept = jnp.where(my_core == 0, layers[0], layers[1])
    received = swapped(jnp.where(my_core == 0, layers[1], layers[0]))
    by_core = [jnp.where(my_core == core, kept, received) for core in range(2)]
    return jnp.stack(by_core, axis=2).reshape(1, batches, row_count, features)


def solution(mesh):
    return jax.shard_map(
        body,
        mesh=mesh,
        in_specs=(
            P(None, "expert", None),
            P("section", None, None, None),
            P("section", None, "expert", None),
            P("section", "expert", None, None),
            P("section", "expert", None, None),
            P("section", "expert", None, None),
        ),
        out_specs=P("section", None, "expert", None),
        check_vma=False,
    )
```

```python
import functools

import jax
import jax.numpy as jnp
from jax import lax
from jax.experimental import pallas as pl
from jax.experimental.pallas import tpu as pltpu
from jax.sharding import PartitionSpec as P

epsilon = 1e-06
group = 1
unrolled_experts = 8


def load_kernel(*refs):
    count = len(refs) // 2
    sources, places = refs[:count], refs[count:]

    def inner(arrived):
        copies = [pltpu.make_async_copy(sources[i], places[i], arrived.at[i]) for i in range(count)]
        for copy in copies:
            copy.start()
        for copy in copies:
            copy.wait()

    pl.run_scoped(inner, pltpu.SemaphoreType.DMA((count,)))


def load_weights(matrices):
    matrices = [pltpu.with_memory_space_constraint(matrix, pltpu.HBM) for matrix in matrices]
    return pl.pallas_call(
        load_kernel,
        in_specs=[pl.BlockSpec(memory_space=pltpu.HBM)] * len(matrices),
        out_specs=[pl.BlockSpec(memory_space=pltpu.VMEM)] * len(matrices),
        out_shape=[jax.ShapeDtypeStruct(matrix.shape, matrix.dtype) for matrix in matrices],
        compiler_params=pltpu.CompilerParams(vmem_limit_bytes=10 << 20),
        cost_estimate=pl.CostEstimate(flops=0, bytes_accessed=sum(m.size for m in matrices) * 2, transcendentals=0),
        name="load_weights",
    )(*matrices)


def mlp_kernel(
    pick_ref, own_ref, other_ref, weight_ref, gate_0, up_0, down_0, gate_1, up_1, down_1, keep_ref, give_ref, normed_ref
):
    half = own_ref.shape[0]
    for side, rows_ref in enumerate((own_ref, other_ref)):
        widened = rows_ref[...].astype(jnp.float32)
        inverse_rms = lax.rsqrt(jnp.mean(widened * widened, axis=-1, keepdims=True) + epsilon)
        normed_ref[side * half : (side + 1) * half, :] = (widened * inverse_rms).astype(jnp.bfloat16)

    def with_weights(gate_ref, up_ref, down_ref):
        gate_part = jnp.dot(normed_ref[...], gate_ref[...], preferred_element_type=jnp.float32)
        up_part = jnp.dot(normed_ref[...], up_ref[...], preferred_element_type=jnp.float32)
        activated = (gate_part / (1.0 + jnp.exp(-gate_part)) * up_part).astype(jnp.bfloat16)
        row_weights = jnp.broadcast_to(weight_ref[pick_ref[0], pick_ref[1]], (128, 2 * half)).T[:, :1]
        weighted = jnp.dot(activated, down_ref[...], preferred_element_type=jnp.float32) * row_weights
        keep_ref[...] = weighted[:half].astype(jnp.bfloat16)
        give_ref[...] = weighted[half:].astype(jnp.bfloat16)

    @pl.when(pick_ref[0] == 0)
    def _():
        with_weights(gate_0, up_0, down_0)

    @pl.when(pick_ref[0] == 1)
    def _():
        with_weights(gate_1, up_1, down_1)


def expert_mlp(pick, own, other, token_weights, matrices):
    half, features = own.shape
    rows = 2 * half
    hidden = matrices[0].shape[1]
    in_vmem = pl.BlockSpec(memory_space=pltpu.VMEM)
    return pl.pallas_call(
        mlp_kernel,
        in_specs=[pl.BlockSpec(memory_space=pltpu.SMEM)] + [in_vmem] * 9,
        out_specs=[in_vmem] * 2,
        out_shape=[jax.ShapeDtypeStruct((half, features), jnp.bfloat16)] * 2,
        scratch_shapes=[pltpu.VMEM((rows, features), jnp.bfloat16)],
        compiler_params=pltpu.CompilerParams(vmem_limit_bytes=(8 << 20) + 28 * rows * features),
        cost_estimate=pl.CostEstimate(
            flops=6 * rows * features * hidden, bytes_accessed=6 * features * hidden, transcendentals=rows * hidden
        ),
        name="expert_mlp",
    )(pick, own, other, token_weights, *matrices)


def body(tokens_in, expert_ids, gate_values, expert_gate, expert_up, expert_down):
    sections = lax.axis_size("section")
    section_now = lax.axis_index("section")
    experts = lax.axis_size("expert")
    my_expert = lax.axis_index("expert")
    planes = sections // 2
    my_plane, my_core = section_now // 2, section_now % 2
    columns = experts // 2
    my_column, my_side = my_expert // 2, my_expert % 2
    batches, row_count, features = tokens_in.shape
    block = group * row_count
    half = columns * block
    rounds = batches // (2 * group)
    pairs = rounds // 2

    def swapped(value):
        return lax.ppermute(value, "section", [(s, s ^ 1) for s in range(sections)])

    own_matrices = (expert_gate[0, 0], expert_up[0, 0], expert_down[0, 0])
    matrices = (*own_matrices, *load_weights([swapped(matrix) for matrix in own_matrices]))
    matrices = tuple(pltpu.with_memory_space_constraint(matrix, pltpu.VMEM) for matrix in matrices)

    my_routes = lax.dynamic_slice_in_dim(expert_ids[0], my_expert * row_count, row_count, 1)
    named = my_routes[None] == jnp.arange(experts, dtype=jnp.int32)[:, None, None, None]
    token_weights = jnp.sum(jnp.where(named, gate_values[0][None], 0.0), axis=3)
    token_weights = lax.all_to_all(token_weights, "expert", split_axis=0, concat_axis=0, tiled=True)
    apart = jnp.arange(columns, dtype=jnp.int32)
    sources = (my_column - apart) % columns * 2
    order = jnp.concatenate([sources + my_side, sources + 1 - my_side])
    token_weights = token_weights[order].reshape(experts, rounds, 2, block).transpose(2, 1, 0, 3)
    token_weights = token_weights.reshape(2, rounds, 1, 2 * half)
    kept = lax.dynamic_index_in_dim(token_weights, my_core, 0, keepdims=False)
    sent = lax.dynamic_index_in_dim(token_weights, 1 - my_core, 0, keepdims=False)
    token_weights = jnp.stack([kept, swapped(sent)])

    fresh_rounds = lax.dynamic_index_in_dim(
        tokens_in.reshape(rounds, 2, block, features), my_core, 1, keepdims=False
    )

    def along_columns(value, apart, planes_on):
        route = []
        for section in range(sections):
            for e in range(experts):
                target = (section + 2 * planes_on) % sections * experts + (e // 2 + apart) % columns * 2 + e % 2
                route.append((section * experts + e, target))
        return lax.ppermute(value, ("section", "expert"), route)

    def across(value):
        return lax.ppermute(value, "expert", [(e, e ^ 1) for e in range(experts)])

    def added(*terms):
        return functools.reduce(jnp.add, [term.astype(jnp.float32) for term in terms])

    def one_slot(opening, closing):
        opened = result = None
        if closing is not None:
            own, other, layer, round_now = closing
            pick = jnp.stack([(layer + my_core) % 2, round_now]).astype(jnp.int32)
            keep, give = expert_mlp(pick, own, other, token_weights, matrices)
        if opening is not None:
            payload, from_before = opening
            if closing is not None:
                give, payload = lax.optimization_barrier((give, payload))
            first = along_columns(payload, 0, 1) if from_before else payload
            gathered = [first] + [along_columns(payload, d, int(from_before)) for d in range(1, columns)]
        if closing is not None:
            summed = added(keep, across(give)).astype(jnp.bfloat16).reshape(columns, block, features)
            returned = [along_columns(summed[d], -d, 0) for d in range(1, columns)]
            result = added(own[:block], summed[0], *returned).astype(jnp.bfloat16)
        if opening is not None:
            own_column = jnp.concatenate(gathered, axis=0)
            opened = (own_column, across(own_column))
        return opened, result

    steps = planes + pairs - 1

    def one_step(step, result_a, second_b, first=False):
        pair = jnp.clip(step - my_plane, 0, pairs - 1)
        pair_before = jnp.clip(step - 1 - my_plane, 0, pairs - 1)
        entering = jnp.minimum(step, pairs - 1) * 2
        fresh = [lax.dynamic_index_in_dim(fresh_rounds, entering + i, 0, keepdims=False) for i in range(2)]

        def payload(rows, i):
            return fresh[i] if rows is None else jnp.where(my_plane == planes - 1, fresh[i], rows)

        closing = None if first else (*second_b, 1, pair_before * 2 + 1)
        opened_a, last_b = one_slot((payload(result_a, 0), not first), closing)
        opened_b, first_a = one_slot((payload(last_b, 1), not first), (*opened_a, 0, pair * 2))
        opened_a, first_b = one_slot((first_a, False), (*opened_b, 0, pair * 2 + 1))
        opened_b, last_a = one_slot((first_b, False), (*opened_a, 1, pair * 2))
        return (first_a, last_a, first_b, last_b), opened_b

    if experts <= unrolled_experts:
        history, result_a, second_b = [], None, None
        for step in range(steps):
            results, second_b = one_step(step, result_a, second_b, step == 0)
            result_a = results[1]
            history.append(results)
        last_b = one_slot(None, (*second_b, 1, pairs * 2 - 1))[1]
        late_b = [results[3] for results in history[1:]] + [last_b]
        history = [jnp.stack(part) for part in (*list(zip(*history))[:3], late_b)]
    else:
        blank, rows_blank = jnp.zeros((half, features), jnp.bfloat16), jnp.zeros((block, features), jnp.bfloat16)

        def looped(step, carried):
            results, second_b = one_step(step, *carried[:2])
            history = [lax.dynamic_update_index_in_dim(h, r, step, 0) for h, r in zip(carried[2], results)]
            return results[1], second_b, history

        kept = [jnp.zeros((steps + 1, block, features), jnp.bfloat16)] * 4
        carried = lax.fori_loop(0, steps + 1, looped, (rows_blank, (blank, blank), kept))
        history = [h[:-1] for h in carried[2][:3]] + [carried[2][3][1:]]
    history = [lax.dynamic_slice_in_dim(h, my_plane, pairs, 0) for h in history]
    layers = [jnp.stack([history[i], history[i + 2]], axis=1) for i in range(2)]
    kept = jnp.where(my_core == 0, layers[0], layers[1])
    received = swapped(jnp.where(my_core == 0, layers[1], layers[0]))
    by_core = [jnp.where(my_core == core, kept, received) for core in range(2)]
    return jnp.stack(by_core, axis=2).reshape(1, batches, row_count, features)


def solution(mesh):
    return jax.shard_map(
        body,
        mesh=mesh,
        in_specs=(
            P(None, "expert", None),
            P("section", None, None, None),
            P("section", None, "expert", None),
            P("section", "expert", None, None),
            P("section", "expert", None, None),
            P("section", "expert", None, None),
        ),
        out_specs=P("section", None, "expert", None),
        check_vma=False,
    )
```

```python
import functools

import jax
import jax.numpy as jnp
from jax import lax
from jax.experimental import pallas as pl
from jax.experimental.pallas import tpu as pltpu
from jax.sharding import PartitionSpec as P

epsilon = 1e-06
group = 2
unrolled_experts = 8


def load_kernel(core_ref, *refs):
    count = len(refs) // 4
    own, swapped, layers = refs[:count], refs[count : 2 * count], refs[2 * count :]

    def inner(arrived):
        def copied(sources):
            copies = [pltpu.make_async_copy(sources[i], layers[i], arrived.at[i]) for i in range(2 * count)]
            for copy in copies:
                copy.start()
            for copy in copies:
                copy.wait()

        @pl.when(core_ref[0] == 0)
        def _():
            copied(own + swapped)

        @pl.when(core_ref[0] == 1)
        def _():
            copied(swapped + own)

    pl.run_scoped(inner, pltpu.SemaphoreType.DMA((2 * count,)))


def load_weights(core, own, swapped):
    matrices = [pltpu.with_memory_space_constraint(matrix, pltpu.HBM) for matrix in (*own, *swapped)]
    return pl.pallas_call(
        load_kernel,
        in_specs=[pl.BlockSpec(memory_space=pltpu.SMEM)] + [pl.BlockSpec(memory_space=pltpu.HBM)] * len(matrices),
        out_specs=[pl.BlockSpec(memory_space=pltpu.VMEM)] * len(matrices),
        out_shape=[jax.ShapeDtypeStruct(matrix.shape, matrix.dtype) for matrix in matrices],
        compiler_params=pltpu.CompilerParams(vmem_limit_bytes=20 << 20),
        cost_estimate=pl.CostEstimate(flops=0, bytes_accessed=sum(m.size for m in matrices) * 2, transcendentals=0),
        name="load_weights",
    )(core, *matrices)


def mlp_kernel(offset, pick_ref, own_ref, other_ref, weight_ref, gate_ref, up_ref, down_ref, keep_ref, give_ref, normed_ref):
    half = own_ref.shape[0]
    for side, rows_ref in enumerate((own_ref, other_ref)):
        widened = rows_ref[...].astype(jnp.float32)
        inverse_rms = lax.rsqrt(jnp.mean(widened * widened, axis=-1, keepdims=True) + epsilon)
        normed_ref[side * half : (side + 1) * half, :] = (widened * inverse_rms).astype(jnp.bfloat16)
    gate_part = jnp.dot(normed_ref[...], gate_ref[...], preferred_element_type=jnp.float32)
    up_part = jnp.dot(normed_ref[...], up_ref[...], preferred_element_type=jnp.float32)
    activated = (gate_part / (1.0 + jnp.exp(-gate_part)) * up_part).astype(jnp.bfloat16)
    place, part = offset
    row_weights = weight_ref[pick_ref[place], pick_ref[place + 1] + part]
    row_weights = jnp.broadcast_to(row_weights, (128, 2 * half)).T[:, :1]
    weighted = jnp.dot(activated, down_ref[...], preferred_element_type=jnp.float32) * row_weights
    keep_ref[...] = weighted[:half].astype(jnp.bfloat16)
    give_ref[...] = weighted[half:].astype(jnp.bfloat16)


def expert_mlp(picks, offset, own, other, token_weights, matrices):
    half, features = own.shape
    rows = 2 * half
    hidden = matrices[0].shape[1]
    in_vmem = pl.BlockSpec(memory_space=pltpu.VMEM)
    return pl.pallas_call(
        functools.partial(mlp_kernel, offset),
        in_specs=[pl.BlockSpec(memory_space=pltpu.SMEM)] + [in_vmem] * 6,
        out_specs=[in_vmem] * 2,
        out_shape=[jax.ShapeDtypeStruct((half, features), jnp.bfloat16)] * 2,
        scratch_shapes=[pltpu.VMEM((rows, features), jnp.bfloat16)],
        compiler_params=pltpu.CompilerParams(vmem_limit_bytes=(8 << 20) + 28 * rows * features),
        cost_estimate=pl.CostEstimate(
            flops=6 * rows * features * hidden, bytes_accessed=6 * features * hidden, transcendentals=rows * hidden
        ),
        name="expert_mlp",
    )(picks, own, other, token_weights, *matrices)


def body(tokens_in, expert_ids, gate_values, expert_gate, expert_up, expert_down):
    sections = lax.axis_size("section")
    section_now = lax.axis_index("section")
    experts = lax.axis_size("expert")
    my_expert = lax.axis_index("expert")
    planes = sections // 2
    my_plane, my_core = section_now // 2, section_now % 2
    columns = experts // 2
    my_column, my_side = my_expert // 2, my_expert % 2
    batches, row_count, features = tokens_in.shape
    block = group * row_count
    half = columns * row_count
    rounds = batches // (2 * group)
    pairs = rounds // 2
    steps = planes + pairs - 1

    step_ids = jnp.arange(steps + 1, dtype=jnp.int32)[:, None, None]
    layer_ids = jnp.arange(2, dtype=jnp.int32)[None, :, None]
    stream_ids = jnp.arange(2, dtype=jnp.int32)[None, None, :]
    picked_layer = (layer_ids + my_core) % 2 + 0 * (step_ids + stream_ids)
    picked_batch = (jnp.clip(step_ids - my_plane, 0, pairs - 1) * 2 + stream_ids) * group + 0 * layer_ids
    picks = jnp.stack([picked_layer, picked_batch], axis=-1).astype(jnp.int32).reshape(-1)
    first_core, on_planes = my_core == 0, [my_plane == plane for plane in range(planes)]
    core = my_core.astype(jnp.int32)[None]
    tokens_in, picks, first_core, on_planes, core = lax.optimization_barrier(
        (tokens_in, picks, first_core, on_planes, core)
    )

    def of_core(halves):
        return jnp.where(first_core, halves[0], halves[1]), jnp.where(first_core, halves[1], halves[0])

    def swapped(value):
        return lax.ppermute(value, "section", [(s, s ^ 1) for s in range(sections)])

    own_matrices = (expert_gate[0, 0], expert_up[0, 0], expert_down[0, 0])
    matrices = load_weights(core, own_matrices, [swapped(matrix) for matrix in own_matrices])
    matrices = [pltpu.with_memory_space_constraint(matrix, pltpu.VMEM) for matrix in matrices]
    layer_matrices = (matrices[:3], matrices[3:])

    my_routes = lax.dynamic_slice_in_dim(expert_ids[0], my_expert * row_count, row_count, 1)
    named = my_routes[None] == jnp.arange(experts, dtype=jnp.int32)[:, None, None, None]
    token_weights = jnp.sum(jnp.where(named, gate_values[0][None], 0.0), axis=3)
    token_weights = lax.all_to_all(token_weights, "expert", split_axis=0, concat_axis=0, tiled=True)
    sources = (my_column - jnp.arange(columns, dtype=jnp.int32)) % columns * 2
    order = jnp.concatenate([sources + my_side, sources + 1 - my_side])
    token_weights = token_weights[order].reshape(experts, rounds, 2, group, row_count).transpose(2, 1, 3, 0, 4)
    token_weights = token_weights.reshape(2, rounds * group, 1, experts * row_count)
    kept, sent = of_core(token_weights)
    token_weights = jnp.stack([kept, swapped(sent)])

    tokens_by_core = tokens_in.reshape(rounds, 2, block, features)
    fresh_rounds = of_core((tokens_by_core[:, 0], tokens_by_core[:, 1]))[0]

    def along_columns(value, apart, planes_on):
        route = []
        for section in range(sections):
            for e in range(experts):
                target = (section + 2 * planes_on) % sections * experts + (e // 2 + apart) % columns * 2 + e % 2
                route.append((section * experts + e, target))
        return lax.ppermute(value, ("section", "expert"), route)

    def across(value):
        return lax.ppermute(value, "expert", [(e, e ^ 1) for e in range(experts)])

    def added(*terms):
        return functools.reduce(jnp.add, [term.astype(jnp.float32) for term in terms])

    def batches_of(rows):
        return [rows[m * row_count : (m + 1) * row_count] for m in range(group)]

    def one_slot(opening, closing):
        opened = result = None
        if closing is not None:
            residual, gathered, step, layer, stream = closing
            place = ((step * 2 + layer) * 2 + stream) * 2
            slot_picks = picks
            if not isinstance(place, int):
                slot_picks, place = lax.dynamic_slice_in_dim(picks, place, 2), 0
            keep, give = [], []
            for m, (own, other) in enumerate(gathered):
                kept, given = expert_mlp(slot_picks, (place, m), own, other, token_weights, layer_matrices[layer])
                keep.append(kept)
                give.append(given)
        if opening is not None:
            payload, from_before = opening
            if closing is not None:
                payload, give = lax.optimization_barrier((payload, give))
            first = along_columns(payload, 0, 1) if from_before else payload
            column = [first] + [along_columns(payload, d, int(from_before)) for d in range(1, columns)]
        if closing is not None:
            summed = [added(kept, across(given)).astype(jnp.bfloat16) for kept, given in zip(keep, give)]
            parts_back = [[part[d * row_count : (d + 1) * row_count] for d in range(columns)] for part in summed]
            if opening is not None:
                parts_back = [[jnp.concatenate(blocks) for blocks in zip(*parts_back)]]
            result = []
            for m, blocks in enumerate(parts_back):
                size = blocks[0].shape[0]
                returned = [along_columns(blocks[d], -d, 0) for d in range(1, columns)]
                rows = residual[m * size : (m + 1) * size]
                result.append(added(rows, blocks[0], *returned).astype(jnp.bfloat16))
            result = jnp.concatenate(result)
        if opening is not None:
            owns = [jnp.concatenate(rows) for rows in zip(*[batches_of(rows) for rows in column])]
            opened = (first, [(own, across(own)) for own in owns])
        return opened, result

    def one_step(step, fresh, result_a, second_b, first=False):
        def payload(rows, i):
            return fresh[i] if rows is None else jnp.where(on_planes[-1], fresh[i], rows)

        closing = None if first else (*second_b, step - 1, 1, 1)
        opened_a, last_b = one_slot((payload(result_a, 0), not first), closing)
        opened_b, first_a = one_slot((payload(last_b, 1), not first), (*opened_a, step, 0, 0))
        opened_a, first_b = one_slot((first_a, False), (*opened_b, step, 0, 1))
        opened_b, last_a = one_slot((first_b, False), (*opened_a, step, 1, 0))
        return (first_a, last_a, first_b, last_b), opened_b

    if experts <= unrolled_experts:
        history, result_a, second_b = [], None, None
        for step in range(steps):
            entering = min(step, pairs - 1) * 2
            fresh = [fresh_rounds[entering + i] for i in range(2)]
            results, second_b = one_step(step, fresh, result_a, second_b, step == 0)
            result_a = results[1]
            history.append(results)
        last_b = one_slot(None, (*second_b, steps - 1, 1, 1))[1]
        late_b = [results[3] for results in history[1:]] + [last_b]
        history = [jnp.stack(part) for part in (*list(zip(*history))[:3], late_b)]
    else:
        blank, rows_blank = jnp.zeros((half, features), jnp.bfloat16), jnp.zeros((block, features), jnp.bfloat16)

        def looped(step, carried):
            entering = jnp.minimum(step, pairs - 1) * 2
            fresh = [lax.dynamic_index_in_dim(fresh_rounds, entering + i, 0, keepdims=False) for i in range(2)]
            results, second_b = one_step(step, fresh, *carried[:2])
            history = [lax.dynamic_update_index_in_dim(h, r, step, 0) for h, r in zip(carried[2], results)]
            return results[1], second_b, history

        kept = [jnp.zeros((steps + 1, block, features), jnp.bfloat16)] * 4
        blank_b = (rows_blank, [(blank, blank)] * group)
        carried = lax.fori_loop(0, steps + 1, looped, (rows_blank, blank_b, kept))
        history = [h[:-1] for h in carried[2][:3]] + [carried[2][3][1:]]
    history = [
        functools.reduce(lambda rows, plane: jnp.where(on_planes[plane], h[plane : plane + pairs], rows), range(1, planes), h[:pairs])
        for h in history
    ]
    layers = [jnp.stack([history[i], history[i + 2]], axis=1) for i in range(2)]
    kept, sent = of_core(layers)
    by_core = of_core((kept, swapped(sent)))
    return jnp.stack(by_core, axis=2).reshape(1, batches, row_count, features)


def solution(mesh):
    return jax.shard_map(
        body,
        mesh=mesh,
        in_specs=(
            P(None, "expert", None),
            P("section", None, None, None),
            P("section", None, "expert", None),
            P("section", "expert", None, None),
            P("section", "expert", None, None),
            P("section", "expert", None, None),
        ),
        out_specs=P("section", None, "expert", None),
        check_vma=False,
    )
```

```python
import functools

import jax
import jax.numpy as jnp
from jax import lax
from jax.experimental import pallas as pl
from jax.experimental.pallas import tpu as pltpu
from jax.sharding import PartitionSpec as P

epsilon = 1e-06
group = 2
unrolled_experts = 8


def load_kernel(swap_ref, *refs):
    count = len(refs) // 3
    own, swapped, places = refs[:count], refs[count : 2 * count], refs[2 * count :]

    def inner(arrived):
        def copied(sources):
            copies = [pltpu.make_async_copy(sources[i], places[i], arrived.at[i]) for i in range(count)]
            for copy in copies:
                copy.start()
            for copy in copies:
                copy.wait()

        @pl.when(swap_ref[0] == 0)
        def _():
            copied(own)

        @pl.when(swap_ref[0] == 1)
        def _():
            copied(swapped)

    pl.run_scoped(inner, pltpu.SemaphoreType.DMA((count,)))


def load_weights(swap, own, swapped):
    matrices = [pltpu.with_memory_space_constraint(matrix, pltpu.HBM) for matrix in (*own, *swapped)]
    return pl.pallas_call(
        load_kernel,
        in_specs=[pl.BlockSpec(memory_space=pltpu.SMEM)] + [pl.BlockSpec(memory_space=pltpu.HBM)] * len(matrices),
        out_specs=[pl.BlockSpec(memory_space=pltpu.VMEM)] * len(own),
        out_shape=[jax.ShapeDtypeStruct(matrix.shape, matrix.dtype) for matrix in own],
        compiler_params=pltpu.CompilerParams(vmem_limit_bytes=10 << 20),
        cost_estimate=pl.CostEstimate(flops=0, bytes_accessed=sum(m.size for m in own) * 2, transcendentals=0),
        name="load_weights",
    )(swap, *matrices)


def mlp_kernel(offset, pick_ref, own_ref, other_ref, weight_ref, gate_ref, up_ref, down_ref, keep_ref, give_ref, normed_ref):
    half = own_ref.shape[0]
    for side, rows_ref in enumerate((own_ref, other_ref)):
        widened = rows_ref[...].astype(jnp.float32)
        inverse_rms = lax.rsqrt(jnp.mean(widened * widened, axis=-1, keepdims=True) + epsilon)
        normed_ref[side * half : (side + 1) * half, :] = (widened * inverse_rms).astype(jnp.bfloat16)
    gate_part = jnp.dot(normed_ref[...], gate_ref[...], preferred_element_type=jnp.float32)
    up_part = jnp.dot(normed_ref[...], up_ref[...], preferred_element_type=jnp.float32)
    activated = (gate_part / (1.0 + jnp.exp(-gate_part)) * up_part).astype(jnp.bfloat16)
    place, part = offset
    row_weights = weight_ref[pick_ref[place], pick_ref[place + 1] + part]
    row_weights = jnp.broadcast_to(row_weights, (128, 2 * half)).T[:, :1]
    weighted = jnp.dot(activated, down_ref[...], preferred_element_type=jnp.float32) * row_weights
    keep_ref[...] = weighted[:half].astype(jnp.bfloat16)
    give_ref[...] = weighted[half:].astype(jnp.bfloat16)


def expert_mlp(picks, offset, own, other, token_weights, matrices):
    half, features = own.shape
    rows = 2 * half
    hidden = matrices[0].shape[1]
    in_vmem = pl.BlockSpec(memory_space=pltpu.VMEM)
    return pl.pallas_call(
        functools.partial(mlp_kernel, offset),
        in_specs=[pl.BlockSpec(memory_space=pltpu.SMEM)] + [in_vmem] * 6,
        out_specs=[in_vmem] * 2,
        out_shape=[jax.ShapeDtypeStruct((half, features), jnp.bfloat16)] * 2,
        scratch_shapes=[pltpu.VMEM((rows, features), jnp.bfloat16)],
        compiler_params=pltpu.CompilerParams(vmem_limit_bytes=(8 << 20) + 28 * rows * features),
        cost_estimate=pl.CostEstimate(
            flops=6 * rows * features * hidden, bytes_accessed=6 * features * hidden, transcendentals=rows * hidden
        ),
        name="expert_mlp",
    )(picks, own, other, token_weights, *matrices)


def body(tokens_in, expert_ids, gate_values, expert_gate, expert_up, expert_down):
    sections = lax.axis_size("section")
    section_now = lax.axis_index("section")
    experts = lax.axis_size("expert")
    my_expert = lax.axis_index("expert")
    planes = sections // 2
    my_plane, my_core = section_now // 2, section_now % 2
    columns = experts // 2
    my_column, my_side = my_expert // 2, my_expert % 2
    batches, row_count, features = tokens_in.shape
    block = group * row_count
    half = columns * row_count
    rounds = batches // (2 * group)
    pairs = rounds // 2
    steps = planes + pairs - 1

    step_ids = jnp.arange(steps + 1, dtype=jnp.int32)[:, None, None]
    layer_ids = jnp.arange(2, dtype=jnp.int32)[None, :, None]
    stream_ids = jnp.arange(2, dtype=jnp.int32)[None, None, :]
    picked_layer = (layer_ids + my_core) % 2 + 0 * (step_ids + stream_ids)
    picked_batch = (jnp.clip(step_ids - my_plane, 0, pairs - 1) * 2 + stream_ids) * group + 0 * layer_ids
    picks = jnp.stack([picked_layer, picked_batch], axis=-1).astype(jnp.int32).reshape(-1)
    first_core, on_planes = my_core == 0, [my_plane == plane for plane in range(planes)]
    cores = [my_core.astype(jnp.int32)[None], (1 - my_core).astype(jnp.int32)[None]]
    tokens_in, picks, first_core, on_planes, cores = lax.optimization_barrier(
        (tokens_in, picks, first_core, on_planes, cores)
    )

    def of_core(halves):
        return jnp.where(first_core, halves[0], halves[1]), jnp.where(first_core, halves[1], halves[0])

    def swapped(value):
        return lax.ppermute(value, "section", [(s, s ^ 1) for s in range(sections)])

    own_matrices = (expert_gate[0, 0], expert_up[0, 0], expert_down[0, 0])
    swapped_matrices = [swapped(matrix) for matrix in own_matrices]
    layer_matrices = [
        [
            pltpu.with_memory_space_constraint(matrix, pltpu.VMEM)
            for matrix in load_weights(swap, own_matrices, swapped_matrices)
        ]
        for swap in cores
    ]

    my_routes = lax.dynamic_slice_in_dim(expert_ids[0], my_expert * row_count, row_count, 1)
    named = my_routes[None] == jnp.arange(experts, dtype=jnp.int32)[:, None, None, None]
    token_weights = jnp.sum(jnp.where(named, gate_values[0][None], 0.0), axis=3)
    token_weights = token_weights.reshape(experts, 1, batches * row_count)
    token_weights = lax.all_to_all(token_weights, "expert", split_axis=0, concat_axis=0, tiled=True)

    def weights_of_layers(token_weights):
        sources = (my_column - jnp.arange(columns, dtype=jnp.int32)) % columns * 2
        order = jnp.concatenate([sources + my_side, sources + 1 - my_side])
        token_weights = token_weights[order].reshape(experts, rounds, 2, group, row_count).transpose(2, 1, 3, 0, 4)
        token_weights = token_weights.reshape(2, rounds * group, 1, experts * row_count)
        kept, sent = of_core(token_weights)
        return jnp.stack([kept, swapped(sent)])

    tokens_by_core = tokens_in.reshape(rounds, 2, block, features)
    fresh_rounds = of_core((tokens_by_core[:, 0], tokens_by_core[:, 1]))[0]

    def along_columns(value, apart, planes_on):
        route = []
        for section in range(sections):
            for e in range(experts):
                target = (section + 2 * planes_on) % sections * experts + (e // 2 + apart) % columns * 2 + e % 2
                route.append((section * experts + e, target))
        return lax.ppermute(value, ("section", "expert"), route)

    def across(value):
        return lax.ppermute(value, "expert", [(e, e ^ 1) for e in range(experts)])

    def added(*terms):
        return functools.reduce(jnp.add, [term.astype(jnp.float32) for term in terms])

    def batches_of(rows):
        return [rows[m * row_count : (m + 1) * row_count] for m in range(group)]

    def one_slot(opening, closing, token_weights=None):
        opened = result = None
        if closing is not None:
            residual, gathered, step, layer, stream = closing
            place = ((step * 2 + layer) * 2 + stream) * 2
            slot_picks = picks
            if not isinstance(place, int):
                slot_picks, place = lax.dynamic_slice_in_dim(picks, place, 2), 0
            keep, give = [], []
            for m, (own, other) in enumerate(gathered):
                kept, given = expert_mlp(slot_picks, (place, m), own, other, token_weights, layer_matrices[layer])
                keep.append(kept)
                give.append(given)
        if opening is not None:
            payload, from_before = opening
            if closing is not None:
                payload, give = lax.optimization_barrier((payload, give))
            first = along_columns(payload, 0, 1) if from_before else payload
            column = [first] + [along_columns(payload, d, int(from_before)) for d in range(1, columns)]
        if closing is not None:
            summed = [added(kept, across(given)).astype(jnp.bfloat16) for kept, given in zip(keep, give)]
            parts_back = [[part[d * row_count : (d + 1) * row_count] for d in range(columns)] for part in summed]
            if opening is not None:
                parts_back = [[jnp.concatenate(blocks) for blocks in zip(*parts_back)]]
            result = []
            for m, blocks in enumerate(parts_back):
                size = blocks[0].shape[0]
                returned = [along_columns(blocks[d], -d, 0) for d in range(1, columns)]
                rows = residual[m * size : (m + 1) * size]
                result.append(added(rows, blocks[0], *returned).astype(jnp.bfloat16))
            result = jnp.concatenate(result)
        if opening is not None:
            if closing is None:
                column, token_weights = lax.optimization_barrier((column, token_weights))
                token_weights = weights_of_layers(token_weights)
            owns = [jnp.concatenate(rows) for rows in zip(*[batches_of(rows) for rows in column])]
            opened = (first, [(own, across(own)) for own in owns])
        return opened, result, token_weights

    def one_step(step, fresh, result_a, second_b, weights, first=False):
        def payload(rows, i):
            return fresh[i] if rows is None else jnp.where(on_planes[-1], fresh[i], rows)

        closing = None if first else (*second_b, step - 1, 1, 1)
        opened_a, last_b, weights = one_slot((payload(result_a, 0), not first), closing, weights)
        opened_b, first_a, _ = one_slot((payload(last_b, 1), not first), (*opened_a, step, 0, 0), weights)
        opened_a, first_b, _ = one_slot((first_a, False), (*opened_b, step, 0, 1), weights)
        opened_b, last_a, _ = one_slot((first_b, False), (*opened_a, step, 1, 0), weights)
        return (first_a, last_a, first_b, last_b), opened_b, weights

    if experts <= unrolled_experts:
        history, result_a, second_b, weights = [], None, None, token_weights
        for step in range(steps):
            entering = min(step, pairs - 1) * 2
            fresh = [fresh_rounds[entering + i] for i in range(2)]
            results, second_b, weights = one_step(step, fresh, result_a, second_b, weights, step == 0)
            result_a = results[1]
            history.append(results)
        last_b = one_slot(None, (*second_b, steps - 1, 1, 1), weights)[1]
        late_b = [results[3] for results in history[1:]] + [last_b]
        history = [jnp.stack(part) for part in (*list(zip(*history))[:3], late_b)]
    else:
        blank, rows_blank = jnp.zeros((half, features), jnp.bfloat16), jnp.zeros((block, features), jnp.bfloat16)

        weights = weights_of_layers(token_weights)

        def looped(step, carried):
            entering = jnp.minimum(step, pairs - 1) * 2
            fresh = [lax.dynamic_index_in_dim(fresh_rounds, entering + i, 0, keepdims=False) for i in range(2)]
            results, second_b, _ = one_step(step, fresh, *carried[:2], weights)
            history = [lax.dynamic_update_index_in_dim(h, r, step, 0) for h, r in zip(carried[2], results)]
            return results[1], second_b, history

        kept = [jnp.zeros((steps + 1, block, features), jnp.bfloat16)] * 4
        blank_b = (rows_blank, [(blank, blank)] * group)
        carried = lax.fori_loop(0, steps + 1, looped, (rows_blank, blank_b, kept))
        history = [h[:-1] for h in carried[2][:3]] + [carried[2][3][1:]]
    history = [
        functools.reduce(lambda rows, plane: jnp.where(on_planes[plane], h[plane : plane + pairs], rows), range(1, planes), h[:pairs])
        for h in history
    ]
    layers = [jnp.stack([history[i], history[i + 2]], axis=1) for i in range(2)]
    kept, sent = of_core(layers)
    by_core = of_core((kept, swapped(sent)))
    return jnp.stack(by_core, axis=2).reshape(1, batches, row_count, features)


def solution(mesh):
    return jax.shard_map(
        body,
        mesh=mesh,
        in_specs=(
            P(None, "expert", None),
            P("section", None, None, None),
            P("section", None, "expert", None),
            P("section", "expert", None, None),
            P("section", "expert", None, None),
            P("section", "expert", None, None),
        ),
        out_specs=P("section", None, "expert", None),
        check_vma=False,
    )
```
